256 devices in a mesh: grp: 8 (over z_hi, x), wk: 32 (over z_lo, y, core).
Axes of the slice: x: 4, y: 4, z: 8 (z_hi: 2, z_lo: 4; z = z_hi * 4 + z_lo), core: 2. Of those that a mesh axis runs over, the one named last changes fastest.
Arguments:
- grads: bfloat16 [8, 4, 512, 1024], P('grp', None, 'wk'), may hold values from -4 to 4
- bank: bfloat16 [32, 5, 512, 512], P('wk'), as said below
- owners: int32 [4], replicated, may hold values from 0 to 31, as said below
- col_map: int32 [4, 2], replicated, may hold values from 0 to 3
Outputs:
- update: float32 [4, 512, 1024], P(None, 'grp', 'wk')
The draws below stay inside these ranges and needn't reach their ends.
Inputs may be any that keep to these rules, and one draw needn't show every extreme that they name: `owners`: 4 distinct worker indices; the last worker serves one of the layers. `bank`: every block is symmetric.
All inputs are finite; a program needn't handle non-finite values.
Results may differ from the reference program's by a relative error of at most 0.015.
Values may be sent and summed in bfloat16 or wider, within the bound.
A program may use at most 64 MiB of HBM per device.

```python
import math
import jax
import jax.numpy as jnp
from jax import lax

B = 512
COLB = 2
OUTB = 4
LAYERS = 4
WIDTH = 1024
N_GRP = 8
N_WK = 32


def draw_bank(key, part):
    first_key = jax.random.fold_in(key, 11)
    second_key = jax.random.fold_in(key, 23)
    shape = (N_WK, OUTB + 1, B, B)
    raw = jax.random.normal(first_key, shape, jnp.float32) * 0.6
    diagonal = jnp.exp(jax.random.uniform(second_key, (N_WK, OUTB + 1, B), jnp.float32, math.log(0.5), math.log(2.0)))
    symmetric = (raw + jnp.swapaxes(raw, -1, -2)) * (0.7071 / math.sqrt(B))
    identity = jnp.eye(B, dtype=jnp.float32)
    return (symmetric * (1.0 - identity) + identity * diagonal[..., None]).astype(jnp.bfloat16)


def draw_owners(key, part):
    first_key = jax.random.fold_in(key, 31)
    second_key = jax.random.fold_in(key, 47)
    others = jax.random.permutation(first_key, N_WK - 1)[:LAYERS - 1].astype(jnp.int32)
    values = jnp.concatenate([others, jnp.full((1,), N_WK - 1, jnp.int32)])
    order = jax.random.permutation(second_key, LAYERS).astype(jnp.int32)
    return values[order].astype(jnp.int32)


def with_ends(drawn, key, low, top_value):
    shape = drawn.shape
    place = [jax.random.randint(jax.random.fold_in(key, axis), (), 0, shape[axis]) for axis in range(len(shape))]
    drawn = drawn.at[tuple(place)].set(low)
    longest = shape.index(max(shape))
    place[longest] = (place[longest] + 1) % shape[longest]
    return drawn.at[tuple(place)].set(top_value)


def shard_levels(own_key, extent, split, smallest, top_value):
    factor_of, own = 1.0, jax.random.fold_in(own_key, 6)
    for axis_at, shards_of in split:
        heights = jnp.exp(jax.random.uniform(jax.random.fold_in(own, axis_at), (shards_of,), jnp.float32, smallest / len(split), top_value / len(split)))
        factor_of = factor_of * jnp.repeat(heights, extent[axis_at] // shards_of).reshape([-1 if axis == axis_at else 1 for axis in range(len(extent))])
    return factor_of


def noise(key, shape, width, most, shards=(), kind=jnp.bfloat16):
    gain = shard_levels(key, shape, shards, -0.22, 0.18) if shards else 1.0
    entries = jax.random.normal(key, shape, jnp.float32) * width * gain
    return jnp.minimum(jnp.maximum(entries, -most), most).astype(kind)


def setup_inputs(seed: int = 0) -> dict:
    keys = jax.random.split(jax.random.key(seed), 5)
    return {
        "grads": noise(keys[0], (N_GRP, LAYERS, B, WIDTH), 0.5, 4.0, ((0, 8), (2, 32))),
        "bank": draw_bank(jax.random.fold_in(keys[4], 71), 0),
        "owners": draw_owners(jax.random.fold_in(keys[4], 71), 0),
        "col_map": with_ends(jax.random.randint(keys[3], (LAYERS, COLB), 0, OUTB), jax.random.fold_in(keys[3], 1), 0, OUTB - 1).astype(jnp.int32),
    }


def right_multiply(rows_in, right_blocks):
    rows_count = rows_in.shape[0]
    split_rows = rows_in.astype(jnp.float32).reshape(rows_count, COLB, B)
    mixed = jnp.einsum("nkb,kbc->nkc", split_rows, right_blocks.astype(jnp.float32))
    return mixed.reshape(rows_count, COLB * B).astype(jnp.bfloat16)


def reference(grads, bank, owners, col_map):
    results = []
    for layer_index in range(LAYERS):
        factors = bank[owners[layer_index]]
        left_inverse = factors[0]
        right_blocks = jnp.take(factors[1:], col_map[layer_index], axis=0)
        summed = jnp.sum(grads[:, layer_index].astype(jnp.float32), axis=0).astype(jnp.bfloat16)
        summed = lax.optimization_barrier(summed)
        mixed = right_multiply(summed, right_blocks)
        results.append(jnp.dot(left_inverse, mixed, preferred_element_type=jnp.float32))
    return jnp.stack(results)
```

```python
import functools

import jax
import jax.numpy as jnp
from jax import lax
from jax.experimental import pallas as pl
from jax.experimental.pallas import tpu as pltpu
from jax.sharding import PartitionSpec as P

MESH = pl.DeviceIdType.MESH
NZ, NY, NC = 4, 4, 2
NG = 8
B = 512


def kernel(
    owners_ref, cmap_ref, grads_ref, bank_ref, out_ref,
    rx1, s_buf, l_buf, r_all, r_buf, r_tx, u_buf, rx3, p_buf, rx4,
    loc_sem, s1, r1, sz, rz, sy, ry, sc, rc, sf, rf, s3, r3, s4, r4,
):
    g = lax.axis_index("grp")
    w = lax.axis_index("wk")
    z, y, c = w // 8, (w // 2) % 4, w % 2
    l, j = g // 2, g % 2

    def wk(zz, yy, cc):
        return zz * 8 + yy * 2 + cc

    peer = (g, wk(z, y, 1 - c))

    def local(src, dst, sem):
        return pltpu.make_async_copy(src, dst, sem)

    def remote(src, dst, ssem, rsem, dev):
        return pltpu.make_async_remote_copy(
            src_ref=src, dst_ref=dst, send_sem=ssem, recv_sem=rsem,
            device_id=dev, device_id_type=MESH,
        )

    def grad_piece(g2):
        return grads_ref.at[g2 // 2, :, pl.ds(pl.multiple_of((g2 % 2) * B, B), B)]

    cp_g = local(grad_piece(g), rx1.at[NG - 1], loc_sem.at[0])
    cp_l = local(bank_ref.at[0], l_buf.at[c], loc_sem.at[1])
    cp_r = local(bank_ref.at[pl.ds(1, 4)], r_all, loc_sem.at[2])
    cp_g.start()
    cp_l.start()
    cp_r.start()

    barrier = pltpu.get_barrier_semaphore()
    count = 0
    for off in range(NG):
        for zo in range(NZ):
            if off or zo:
                pl.semaphore_signal(
                    barrier, inc=1, device_id=((g + off) % NG, wk((z + zo) % NZ, y, c)), device_id_type=MESH)
                count += 1
    for yo in range(1, NY):
        pl.semaphore_signal(barrier, inc=1, device_id=(g, wk(z, (y + yo) % NY, c)), device_id_type=MESH)
        count += 1
    pl.semaphore_signal(barrier, inc=1, device_id=peer, device_id_type=MESH)
    count += 1
    pl.semaphore_wait(barrier, count)

    sends = []
    first = []
    for off in range(1, NG):
        g2 = (g + off) % NG
        cp = remote(grad_piece(g2), rx1.at[off - 1], s1.at[off - 1], r1.at[off - 1], (g2, w))
        cp.start()
        first.append(cp)
    sends += first

    cp_l.wait()
    f_l = remote(l_buf.at[c], l_buf.at[c], sf.at[0], rf.at[0], peer)
    f_l.start()
    cp_r.wait()
    block = cmap_ref[l, j]
    for zz in range(2):
        for yy in range(NY):
            r_tx[yy, zz] = r_all[block, zz, yy, 1 - c]
    f_r = remote(r_tx, r_buf.at[c], sf.at[1], rf.at[1], peer)
    f_r.start()
    for zz in range(2):
        for yy in range(NY):
            r_buf[c, yy, zz] = r_all[block, zz, yy, c]
    sends += [f_l, f_r]

    cp_g.wait()
    for cp in first:
        cp.wait_recv()
    total = rx1[0].astype(jnp.float32)
    for k in range(1, NG):
        total += rx1[k].astype(jnp.float32)
    s_buf[z, y, c] = total.astype(jnp.bfloat16)

    zs = []
    for off in range(1, NZ):
        cp = remote(s_buf.at[z, y, c], s_buf.at[z, y, c], sz.at[off - 1], rz.at[off - 1],
                    (g, wk((z + off) % NZ, y, c)))
        cp.start()
        zs.append(cp)
    for cp in zs:
        cp.wait_recv()
    ys = []
    for off in range(1, NY):
        cp = remote(s_buf.at[:, y, c], s_buf.at[:, y, c], sy.at[off - 1], ry.at[off - 1],
                    (g, wk(z, (y + off) % NY, c)))
        cp.start()
        ys.append(cp)
    cs = []
    for off in range(NY):
        if off:
            ys[off - 1].wait_recv()
        yy = (y - off + NY) % NY
        cp = remote(s_buf.at[:, yy, c], s_buf.at[:, yy, c], sc.at[off], rc.at[off], peer)
        cp.start()
        cs.append(cp)
    sends += zs + ys + cs
    f_l.wait_recv()
    f_r.wait_recv()
    for cp in cs:
        cp.wait_recv()

    owner = owners_ref[l]
    o_y, o_c = (owner // 2) % 4, owner % 2
    right = r_buf[o_c].reshape(2 * NY * 32, B)
    summed = s_buf[...].reshape(B, B)
    mixed = lax.dot_general(right, summed, (((1,), (1,)), ((), ())), preferred_element_type=jnp.float32)
    update = jnp.dot(mixed.astype(jnp.bfloat16), l_buf[o_c].reshape(B, B), preferred_element_type=jnp.float32)
    u_buf[...] = update.astype(jnp.bfloat16).reshape(NY, 2, 32, B)

    us = []
    for off in range(1, NY):
        y2 = (y + off) % NY
        cp = remote(u_buf.at[y2], rx3.at[y], s3.at[off - 1], r3.at[off - 1], (g, wk(z, y2, c)))
        cp.start()
        us.append(cp)
    rx3[y] = u_buf[y]
    for cp in us:
        cp.wait_recv()
    sends += us

    low = lax.broadcasted_iota(jnp.int32, (16, 128), 1) < 64
    for zz in range(2):
        for b in range(4):
            top = rx3[o_y, zz, pl.ds(0, 16), pl.ds(128 * b, 128)].astype(jnp.float32)
            bot = rx3[o_y, zz, pl.ds(16, 16), pl.ds(128 * b, 128)].astype(jnp.float32)
            p_buf[zz, 2 * b] = jnp.where(low, top, pltpu.roll(bot, 64, 1)).astype(jnp.bfloat16)
            p_buf[zz, 2 * b + 1] = jnp.where(low, pltpu.roll(top, 64, 1), bot).astype(jnp.bfloat16)
    pending = []
    for zz in range(2):
        z2 = 2 * j + zz
        for off in range(NG):
            g2 = (g + off) % NG
            cp = remote(p_buf.at[zz, g2], rx4.at[l, z], s4.at[zz, off], r4.at[l, z], (g2, wk(z2, y, c)))
            if off:
                cp.start()
                sends.append(cp)
            else:
                own = local(p_buf.at[zz, g2], rx4.at[l, z], r4.at[l, z])

                pl.when(z2 == z)(own.start)
                pl.when(z2 != z)(cp.start)

                pending.append((z2, cp))
    for layer in range(4):
        for zz in range(NZ):
            local(p_buf.at[0, 0], rx4.at[layer, zz], r4.at[layer, zz]).wait()
    for z2, cp in pending:
        pl.when(z2 != z)(cp.wait_send)
    for cp in sends:
        cp.wait_send()
    for layer in range(4):
        out_ref[layer] = rx4[layer, owners_ref[layer] // 8].astype(jnp.float32)


def solution(mesh):
    def step(grads, bank, owners, cmap):
        packed = pl.pallas_call(
            kernel,
            out_shape=jax.ShapeDtypeStruct((4, 16, 128), jnp.float32),
            in_specs=[
                pl.BlockSpec(memory_space=pltpu.SMEM),
                pl.BlockSpec(memory_space=pltpu.SMEM),
                pl.BlockSpec(memory_space=pl.ANY),
                pl.BlockSpec(memory_space=pl.ANY),
            ],
            out_specs=pl.BlockSpec(memory_space=pltpu.VMEM),
            scratch_shapes=[
                pltpu.VMEM((NG, 16, B), jnp.bfloat16),
                pltpu.VMEM((NZ, NY, NC, 16, B), jnp.bfloat16),
                pltpu.VMEM((NC, 2, NY, NC, 32, B), jnp.bfloat16),
                pltpu.VMEM((4, 2, NY, NC, 32, B), jnp.bfloat16),
                pltpu.VMEM((NC, NY, 2, 32, B), jnp.bfloat16),
                pltpu.VMEM((NY, 2, 32, B), jnp.bfloat16),
                pltpu.VMEM((NY, 2, 32, B), jnp.bfloat16),
                pltpu.VMEM((NY, 2, 32, B), jnp.bfloat16),
                pltpu.VMEM((2, NG, 16, 128), jnp.bfloat16),
                pltpu.VMEM((4, NZ, 16, 128), jnp.bfloat16),
                pltpu.SemaphoreType.DMA((3,)),
                pltpu.SemaphoreType.DMA((NG - 1,)),
                pltpu.SemaphoreType.DMA((NG - 1,)),
                pltpu.SemaphoreType.DMA((NZ - 1,)),
                pltpu.SemaphoreType.DMA((NZ - 1,)),
                pltpu.SemaphoreType.DMA((NY - 1,)),
                pltpu.SemaphoreType.DMA((NY - 1,)),
                pltpu.SemaphoreType.DMA((NY,)),
                pltpu.SemaphoreType.DMA((NY,)),
                pltpu.SemaphoreType.DMA((2,)),
                pltpu.SemaphoreType.DMA((2,)),
                pltpu.SemaphoreType.DMA((NY - 1,)),
                pltpu.SemaphoreType.DMA((NY - 1,)),
                pltpu.SemaphoreType.DMA((2, NG)),
                pltpu.SemaphoreType.DMA((4, NZ)),
            ],
            compiler_params=pltpu.CompilerParams(
                collective_id=0, has_side_effects=True, vmem_limit_bytes=32 * 1024 * 1024
            ),
        )(owners, cmap, grads[0], bank.reshape(5, 2, NY, NC, 32, B))
        packed = packed.reshape(4, 16, 2, 64)
        return packed.transpose(0, 3, 2, 1).reshape(4, 64, 32)

    return jax.shard_map(
        step, mesh=mesh,
        in_specs=(P("grp", None, "wk", None), P("wk", None, None, None), P(), P()),
        out_specs=P(None, "grp", "wk"), check_vma=False,
    )
```

```python
import functools

import jax
import jax.numpy as jnp
from jax import lax
from jax.experimental import pallas as pl
from jax.experimental.pallas import tpu as pltpu
from jax.sharding import PartitionSpec as P

MESH = pl.DeviceIdType.MESH
NZ, NY, NC = 4, 4, 2
NG = 8
B = 512


def kernel(
    owners_ref, cmap_ref, grads_ref, bank_ref, out_ref,
    rx1, part_buf, rx2, s_buf, l_buf, r_all, r_buf, r_tx, u_buf, rx3, p_buf, rx4,
    owners_buf, cmap_buf, loc_sem, s1, r1, sz, rz, sy, ry, sc, rc, sf, rf, s3, r3, s4, r4,
):
    g = lax.axis_index("grp")
    w = lax.axis_index("wk")
    z, y, c = w // 8, (w // 2) % 4, w % 2
    h, x = g // 4, g % 4
    l, j = x, h

    def wk(zz, yy, cc):
        return zz * 8 + yy * 2 + cc

    peer = (g, wk(z, y, 1 - c))

    def local(src, dst, sem):
        return pltpu.make_async_copy(src, dst, sem)

    begun, landed = [], []

    def send(src, dst, ssem, rsem, dev):
        copy = pltpu.make_async_remote_copy(
            src_ref=src, dst_ref=dst, send_sem=ssem, recv_sem=rsem,
            device_id=dev, device_id_type=MESH,
        )
        copy.start()
        begun.append(copy)
        return copy

    def arrive(copy):
        copy.wait_recv()
        landed.append(copy)

    def grp(hh, xx):
        return hh * 4 + xx

    cp_g = local(grads_ref.at[x], rx1.at[0], loc_sem.at[0])
    cp_l = local(bank_ref.at[0], l_buf.at[c], loc_sem.at[1])
    cp_r = local(bank_ref.at[pl.ds(1, 4)], r_all, loc_sem.at[2])
    cp_o = local(owners_ref, owners_buf, loc_sem.at[3])
    cp_m = local(cmap_ref, cmap_buf, loc_sem.at[4])
    cp_g.start()
    cp_o.start()
    cp_m.start()
    cp_l.start()
    cp_r.start()

    barrier = pltpu.get_barrier_semaphore()
    mates = [(grp(h, (x + off) % 4), w) for off in range(1, 4)]
    mates += [(grp((h + dh) % 2, x), wk((z + dz) % NZ, y, c)) for dh in range(2) for dz in range(NZ) if dh or dz]
    mates += [(g, wk(z, (y + off) % NY, c)) for off in range(1, NY)]
    mates.append(peer)
    for mate in mates:
        pl.semaphore_signal(barrier, inc=1, device_id=mate, device_id_type=MESH)
    pl.semaphore_wait(barrier, len(mates))

    first = []
    for off in (2, 1, 3):
        x2 = (x + off) % 4
        first.append(send(grads_ref.at[x2], rx1.at[off], s1.at[off], r1.at[off], (grp(h, x2), w)))

    cp_l.wait()
    f_l = send(l_buf.at[c], l_buf.at[c], sf.at[0], rf.at[0], peer)
    cp_r.wait()
    cp_o.wait()
    cp_m.wait()
    block = cmap_buf[j, l]
    for zz in range(2):
        for yy in range(NY):
            r_tx[yy, zz] = r_all[block, zz, yy, 1 - c]
    f_r = send(r_tx, r_buf.at[c], sf.at[1], rf.at[1], peer)
    for zz in range(2):
        for yy in range(NY):
            r_buf[c, yy, zz] = r_all[block, zz, yy, c]

    cp_g.wait()
    for cp in first:
        arrive(cp)
    total = rx1[0].astype(jnp.float32)
    for k in range(1, 4):
        total += rx1[k].astype(jnp.float32)
    total = total.astype(jnp.bfloat16)
    for jj in range(2):
        part_buf[jj] = total[:, jj * B:(jj + 1) * B]
    rx2[h, z] = part_buf[h]

    zs = {}
    for dz in (0, 1, 3, 2):
        for dh in (1, 0):
            if dh or dz:
                h2 = (h + dh) % 2
                zs[dz, dh] = send(part_buf.at[h2], rx2.at[h, z], sz.at[dz, dh], rz.at[dz, dh],
                                  (grp(h2, x), wk((z + dz) % NZ, y, c)))
    ys, cs = [], []

    def pass_on(k, off):
        part = s_buf.at[(z - k + NZ) % NZ, (y - off + NY) % NY, c]
        cs.append(send(part, part, sc.at[k, off], rc.at[k, off], peer))

    for k in (2, 1, 3, 0):
        if k:
            arrive(zs[k, 0])
        arrive(zs[k, 1])
        zz = (z - k + NZ) % NZ
        both = rx2[0, zz].astype(jnp.float32) + rx2[1, zz].astype(jnp.float32)
        s_buf[zz, y, c] = both.astype(jnp.bfloat16)
        part = s_buf.at[zz, y, c]
        for off in (2, 1, 3):
            ys.append((k, off, send(part, part, sy.at[k, off - 1], ry.at[k, off - 1], (g, wk(z, (y + off) % NY, c)))))
        pass_on(k, 0)
    for k, off, cp in ys:
        arrive(cp)
        pass_on(k, off)
    arrive(f_l)
    arrive(f_r)
    for cp in cs:
        arrive(cp)

    owner = owners_buf[l]
    o_y, o_c = (owner // 2) % 4, owner % 2
    right = r_buf[o_c].reshape(2 * NY * 32, B)
    summed = s_buf[...].reshape(B, B)
    mixed = lax.dot_general(right, summed, (((1,), (1,)), ((), ())), preferred_element_type=jnp.float32)
    update = jnp.dot(mixed.astype(jnp.bfloat16), l_buf[o_c].reshape(B, B), preferred_element_type=jnp.float32)
    u_buf[...] = update.astype(jnp.bfloat16).reshape(NY, 2, 32, B)

    us = []
    for off in range(1, NY):
        y2 = (y + off) % NY
        us.append(send(u_buf.at[y2], rx3.at[y], s3.at[off - 1], r3.at[off - 1], (g, wk(z, y2, c))))
    rx3[y] = u_buf[y]
    for cp in us:
        arrive(cp)

    low = lax.broadcasted_iota(jnp.int32, (16, 128), 1) < 64
    for zz in range(2):
        for b in range(4):
            top = rx3[o_y, zz, pl.ds(0, 16), pl.ds(128 * b, 128)].astype(jnp.float32)
            bot = rx3[o_y, zz, pl.ds(16, 16), pl.ds(128 * b, 128)].astype(jnp.float32)
            p_buf[zz, 2 * b] = jnp.where(low, top, pltpu.roll(bot, 64, 1)).astype(jnp.bfloat16)
            p_buf[zz, 2 * b + 1] = jnp.where(low, pltpu.roll(top, 64, 1), bot).astype(jnp.bfloat16)
    kept = []
    for dh, dx in ((1, 2), (1, 1), (1, 3), (1, 0), (0, 2), (0, 1), (0, 3), (0, 0)):
        g2 = grp((h + dh) % 2, (x + dx) % 4)
        for zz in range(2):
            z2 = 2 * j + zz
            k = 4 * dh + dx
            dev = (g2, wk(z2, y, c))
            if k:
                send(p_buf.at[zz, g2], rx4.at[l, z], s4.at[zz, k], r4.at[l, z], dev)
            else:
                own = local(p_buf.at[zz, g2], rx4.at[l, z], r4.at[l, z])
                far = pltpu.make_async_remote_copy(
                    src_ref=p_buf.at[zz, g2], dst_ref=rx4.at[l, z], send_sem=s4.at[zz, k], recv_sem=r4.at[l, z],
                    device_id=dev, device_id_type=MESH)
                pl.when(z2 == z)(own.start)
                pl.when(z2 != z)(far.start)
                kept.append((z2, far))
    for layer in range(4):
        for zz in range(NZ):
            local(p_buf.at[0, 0], rx4.at[layer, zz], r4.at[layer, zz]).wait()
    for z2, far in kept:
        pl.when(z2 != z)(far.wait_send)
    for cp in begun:
        cp.wait_send()
    for layer in range(4):
        tile = rx4[layer, owners_buf[layer] // 8].astype(jnp.float32)
        out_ref[layer, pl.ds(0, 16)] = tile[:, :64]
        out_ref[layer, pl.ds(16, 16)] = pltpu.roll(tile, 64, 1)[:, :64]


def solution(mesh):
    def step(grads, bank, owners, cmap):
        packed = pl.pallas_call(
            kernel,
            out_shape=jax.ShapeDtypeStruct((4, 32, 64), jnp.float32),
            in_specs=[
                pl.BlockSpec(memory_space=pl.ANY),
                pl.BlockSpec(memory_space=pl.ANY),
                pl.BlockSpec(memory_space=pl.ANY),
                pl.BlockSpec(memory_space=pl.ANY),
            ],
            out_specs=pl.BlockSpec(memory_space=pltpu.VMEM),
            scratch_shapes=[
                pltpu.VMEM((4, 16, 2 * B), jnp.bfloat16),
                pltpu.VMEM((2, 16, B), jnp.bfloat16),
                pltpu.VMEM((2, NZ, 16, B), jnp.bfloat16),
                pltpu.VMEM((NZ, NY, NC, 16, B), jnp.bfloat16),
                pltpu.VMEM((NC, 2, NY, NC, 32, B), jnp.bfloat16),
                pltpu.VMEM((4, 2, NY, NC, 32, B), jnp.bfloat16),
                pltpu.VMEM((NC, NY, 2, 32, B), jnp.bfloat16),
                pltpu.VMEM((NY, 2, 32, B), jnp.bfloat16),
                pltpu.VMEM((NY, 2, 32, B), jnp.bfloat16),
                pltpu.VMEM((NY, 2, 32, B), jnp.bfloat16),
                pltpu.VMEM((2, NG, 16, 128), jnp.bfloat16),
                pltpu.VMEM((4, NZ, 16, 128), jnp.bfloat16),
                pltpu.SMEM((4,), jnp.int32),
                pltpu.SMEM((2, 4), jnp.int32),
                pltpu.SemaphoreType.DMA((5,)),
                pltpu.SemaphoreType.DMA((4,)),
                pltpu.SemaphoreType.DMA((4,)),
                pltpu.SemaphoreType.DMA((NZ, 2)),
                pltpu.SemaphoreType.DMA((NZ, 2)),
                pltpu.SemaphoreType.DMA((NZ, NY - 1)),
                pltpu.SemaphoreType.DMA((NZ, NY - 1)),
                pltpu.SemaphoreType.DMA((NZ, NY)),
                pltpu.SemaphoreType.DMA((NZ, NY)),
                pltpu.SemaphoreType.DMA((2,)),
                pltpu.SemaphoreType.DMA((2,)),
                pltpu.SemaphoreType.DMA((NY - 1,)),
                pltpu.SemaphoreType.DMA((NY - 1,)),
                pltpu.SemaphoreType.DMA((2, NG)),
                pltpu.SemaphoreType.DMA((4, NZ)),
            ],
            compiler_params=pltpu.CompilerParams(
                collective_id=0, has_side_effects=True, vmem_limit_bytes=56 * 1024 * 1024
            ),
        )(owners, cmap.T, grads[0], bank.reshape(5, 2, NY, NC, 32, B))
        return packed.transpose(0, 2, 1)

    return jax.shard_map(
        step, mesh=mesh,
        in_specs=(P("grp", None, "wk", None), P("wk", None, None, None), P(), P()),
        out_specs=P(None, "grp", "wk"), check_vma=False,
    )
```
